256 devices in a mesh: row: 16 (over y, x), col: 16 (over z, core).
Axes of the slice: x: 4, y: 4, z: 8, core: 2. Of those that a mesh axis runs over, the one named last changes fastest.
Arguments:
- kernel_matrix: float32 [16384, 16384], P('row', 'col'), may hold values from 0 to 3
Outputs:
- factored: float32 [16384, 16384], P('row', 'col')
The draws below stay inside these ranges and needn't reach their ends.
All inputs are finite; a program needn't handle non-finite values.
Results may differ from the reference program's by a relative error of at most 0.0003.
Values sent between devices are 32-bit elements; how exact they have to be, the bound alone decides.
No kernel may reach another device: no remote copies, remote signals or barrier semaphores. Data moves between devices by JAX's collectives and lax.ppermute only.
A program may use at most 128 MiB of HBM per device.

```python
import jax
import jax.numpy as jnp
from jax import lax

DIM = 28
TILE = 256
ORDER = 16384
STEPS = 3
N_ROW = 16
N_COL = 16


def storage_map(positions, groups):
    per_group = ORDER // (TILE * groups)
    return (positions // TILE % per_group * groups + positions // (per_group * TILE)) * TILE + positions % TILE


def draw_kernel_matrix(key, part):
    key = jax.random.fold_in(key, 11)
    point_key = jax.random.fold_in(key, 0)
    feature_key = jax.random.fold_in(key, 2)
    points = jax.random.normal(point_key, (DIM, ORDER), jnp.float32)
    positions = jnp.arange(ORDER, dtype=jnp.int32)
    row_map = storage_map(positions, N_ROW)
    col_map = storage_map(positions, N_COL)
    row_points = jnp.take(points, row_map, axis=1)
    col_points = jnp.take(points, col_map, axis=1)

    def accumulate(index, total):
        upper = lax.dynamic_index_in_dim(row_points, index, 0, keepdims=False)
        lower = lax.dynamic_index_in_dim(col_points, index, 0, keepdims=False)
        difference = upper[:, None] - lower[None, :]
        return total + difference * difference
    distance = lax.fori_loop(0, DIM, accumulate, jnp.zeros((ORDER, ORDER), jnp.float32))
    features = jax.random.uniform(feature_key, (ORDER, TILE), jnp.float32)
    features = features / jnp.sqrt(jnp.sum(features * features, axis=1, keepdims=True))
    row_features = jnp.take(features, row_map, axis=0)
    col_features = jnp.take(features, col_map, axis=0)
    cosine = jnp.dot(row_features, col_features.T, precision=lax.Precision.HIGHEST, preferred_element_type=jnp.float32)
    same = row_map[:, None] == col_map[None, :]
    cosine = jnp.where(same, 1.0, cosine).astype(jnp.float32)
    identity = jnp.where(same, 1.0, 0.0).astype(jnp.float32)
    return jnp.exp(-distance / DIM) + cosine + identity


def setup_inputs(seed: int = 0) -> dict:
    streams_of = jax.random.split(jax.random.key(seed), 2)
    return {
        "kernel_matrix": draw_kernel_matrix(jax.random.fold_in(streams_of[1], 71), 0),
    }


def reference(kernel_matrix):
    tile_rows = ORDER // (TILE * N_ROW)
    tile_cols = ORDER // (TILE * N_COL)
    matrix = kernel_matrix.reshape(N_ROW, tile_rows, TILE, ORDER).transpose(1, 0, 2, 3).reshape(ORDER, ORDER)
    matrix = matrix.reshape(ORDER, N_COL, tile_cols, TILE).transpose(0, 2, 1, 3).reshape(ORDER, ORDER)
    for panel_step in range(STEPS):
        start_row = panel_step * TILE
        end_row = start_row + TILE
        factor = jnp.linalg.cholesky(matrix[start_row:end_row, start_row:end_row])
        inverse = jax.scipy.linalg.solve_triangular(factor, jnp.eye(TILE, dtype=jnp.float32), lower=True)
        panel = jnp.dot(matrix[end_row:, start_row:end_row].astype(jnp.float32), inverse.T.astype(jnp.float32), precision=lax.Precision.HIGHEST, preferred_element_type=jnp.float32)
        trailing = matrix[end_row:, end_row:] - jnp.dot(panel.astype(jnp.float32), panel.T.astype(jnp.float32), precision=lax.Precision.HIGHEST, preferred_element_type=jnp.float32)
        matrix = matrix.at[end_row:, end_row:].set(trailing)
        matrix = matrix.at[start_row:end_row, start_row:].set(0.0)
        matrix = matrix.at[start_row:end_row, start_row:end_row].set(factor)
        matrix = matrix.at[end_row:, start_row:end_row].set(panel)
    matrix = matrix.reshape(tile_rows, N_ROW, TILE, ORDER).transpose(1, 0, 2, 3).reshape(ORDER, ORDER)
    matrix = matrix.reshape(ORDER, tile_cols, N_COL, TILE).transpose(0, 2, 1, 3).reshape(ORDER, ORDER)
    return matrix
```

```python
import jax
import jax.numpy as jnp
from jax import lax
from jax.experimental import pallas as pl
from jax.experimental.pallas import tpu as pltpu
from jax.sharding import PartitionSpec as P

TILE = 256
STEPS = 3
LEAD = TILE * STEPS
BLOCK = 128
SUB = 8
FULL = lax.Precision.HIGHEST

Y_SIZE, X_SIZE, Z_SIZE = 4, 4, 8
X_GROUPS = [[4 * y + x for x in range(4)] for y in range(4)]
Y_GROUPS = [[4 * y + x for y in range(4)] for x in range(4)]
Z_GROUPS = [[2 * z + core for z in range(8)] for core in range(2)]
CORE_SWAP = [(c, c ^ 1) for c in range(16)]


def dot(left, right, dims, precision=FULL):
    return lax.dot_general(
        left, right, (dims, ((), ())), precision=precision, preferred_element_type=jnp.float32
    )


def spread_row(value, i):
    return jnp.broadcast_to(value[i : i + 1, :], value.shape)


def spread_lane(value, i):
    return jnp.broadcast_to(value[:, i : i + 1], value.shape)


def factor_block(load, store):
    count = BLOCK // SUB
    sub = lax.broadcasted_iota(jnp.int32, (SUB, BLOCK), 0)
    lane = lax.broadcasted_iota(jnp.int32, (SUB, BLOCK), 1)
    left = [load(k) for k in range(count)]
    right = [(lane == sub + SUB * k).astype(jnp.float32) for k in range(count)]
    for k in range(count):
        columns = [spread_lane(left[k], SUB * k + m) for m in range(SUB)]
        s = [[spread_row(columns[m], i) for m in range(SUB)] for i in range(SUB)]
        rows_l = [spread_row(left[k], i) for i in range(SUB)]
        rows_r = [spread_row(right[k], i) for i in range(SUB)]
        out_l, out_r = [None] * SUB, [None] * SUB
        for i in range(SUB):
            scale = lax.rsqrt(s[i][i])
            u = [s[i][n] * scale if n > i else None for n in range(SUB)]
            out_l[i], out_r[i] = rows_l[i] * scale, rows_r[i] * scale
            for m in range(SUB):
                if m == i:
                    continue
                w = u[m] if m > i else s[m][i] * scale
                for n in range(i + 1, SUB):
                    s[m][n] = s[m][n] - w * u[n]
                rows_l[m] = rows_l[m] - w * out_l[i]
                rows_r[m] = rows_r[m] - w * out_r[i]
            for n in range(i + 1, SUB):
                s[i][n] = u[n] * scale
            rows_l[i], rows_r[i] = out_l[i] * scale, out_r[i] * scale
        merged_l, merged_r = out_l[0], out_r[0]
        for i in range(1, SUB):
            merged_l = jnp.where(sub == i, out_l[i], merged_l)
            merged_r = jnp.where(sub == i, out_r[i], merged_r)
        store(k, jnp.where(lane >= sub + SUB * k, merged_l, 0.0), merged_r)
        for j in range(k + 1, count):
            weights = [spread_lane(left[j], SUB * k + m) for m in range(SUB)]
            for m in range(SUB):
                left[j] = left[j] - weights[m] * rows_l[m]
                right[j] = right[j] - weights[m] * rows_r[m]


def factor_kernel(a_ref, u_ref, w_ref, work, block_u, block_w):
    count = LEAD // BLOCK
    work[...] = a_ref[...]
    w_ref[...] = jnp.zeros((LEAD, LEAD), jnp.float32)

    def step(k, carry):
        at = pl.ds(pl.multiple_of(k * BLOCK, BLOCK), BLOCK)

        def load(i):
            return work[pl.ds(pl.multiple_of(k * BLOCK + SUB * i, SUB), SUB), at]

        def store(i, upper, lower):
            block_u[SUB * i : SUB * (i + 1), :] = upper
            block_w[SUB * i : SUB * (i + 1), :] = lower

        factor_block(load, store)
        inverse = block_w[...]
        u_ref[at, :] = dot(inverse, work[at, :], ((1,), (0,)))
        u_ref[at, at] = block_u[...]
        row = lax.broadcasted_iota(jnp.int32, (BLOCK, BLOCK), 0)
        col = lax.broadcasted_iota(jnp.int32, (BLOCK, BLOCK), 1)
        w_ref[at, at] = (row == col).astype(jnp.float32)
        w_ref[at, :] = dot(inverse, w_ref[at, :], ((1,), (0,)))

        def update(i, carry):
            to = pl.ds(pl.multiple_of(i * BLOCK, BLOCK), BLOCK)
            weight = u_ref[at, to]
            work[to, :] = work[to, :] - dot(weight, u_ref[at, :], ((0,), (0,)))
            w_ref[to, :] = w_ref[to, :] - dot(weight, w_ref[at, :], ((0,), (0,)))
            return carry

        lax.fori_loop(k + 1, count, update, 0)
        return carry

    lax.fori_loop(0, count, step, 0)


def factorize(lead):
    shape = jax.ShapeDtypeStruct((LEAD, LEAD), jnp.float32)
    vmem = pl.BlockSpec(memory_space=pltpu.VMEM)
    return pl.pallas_call(
        factor_kernel,
        out_shape=(shape, shape),
        in_specs=[vmem],
        out_specs=(vmem, vmem),
        scratch_shapes=[
            pltpu.VMEM((LEAD, LEAD), jnp.float32),
            pltpu.VMEM((BLOCK, BLOCK), jnp.float32),
            pltpu.VMEM((BLOCK, BLOCK), jnp.float32),
        ],
        compiler_params=pltpu.CompilerParams(vmem_limit_bytes=40 * 2**20),
        cost_estimate=pl.CostEstimate(flops=2 * 10**10, bytes_accessed=10**7, transcendentals=0),
    )(lead)


def gather(value, axis, groups):
    copies = jnp.broadcast_to(value[None], (len(groups[0]),) + value.shape)
    return lax.all_to_all(copies, axis, 0, 0, axis_index_groups=groups)


def choose(index, values, start):
    out = jnp.zeros_like(values[0])
    for i, value in enumerate(values):
        out = jnp.where(index == start + i, value, out)
    return out


def on_device(matrix):
    r = lax.axis_index("row")
    c = lax.axis_index("col")
    y, z, core = r // 4, c // 2, c % 2
    half = 512

    first_cols = matrix[:, :TILE]
    first_rows = matrix[:TILE, :]
    keep = lax.dynamic_slice_in_dim(first_cols, core * half, half, 0)
    give = lax.dynamic_slice_in_dim(first_cols, (1 - core) * half, half, 0)
    got = lax.ppermute(give, "col", CORE_SWAP)
    panel_even = jnp.where(core == 0, keep, got)
    panel_odd = jnp.where(core == 0, got, keep)

    column_quarters = [first_rows[:, TILE * s : TILE * (s + 1)] for s in range(4)]
    corner = matrix[:TILE, :TILE]
    message = [jnp.concatenate([column_quarters[s], corner[64 * s : 64 * (s + 1)]]) for s in range(4)]
    arrived = [
        lax.ppermute(message[s], "row", [(x, 4 * s + x) for x in range(3)]) for s in range(1, 4)
    ]
    mine = choose(y, [message[0]] + arrived, 0)
    my_quarter, my_corner = mine[:TILE], mine[TILE:]

    keep = lax.dynamic_slice_in_dim(my_corner, core * 32, 32, 0)
    give = lax.dynamic_slice_in_dim(my_corner, (1 - core) * 32, 32, 0)
    got = lax.ppermute(give, "col", CORE_SWAP)
    even = jnp.where(core == 0, keep, got)
    odd = jnp.where(core == 0, got, keep)
    pair = jnp.stack([even, odd])
    across = lax.ppermute(pair, "col", [(0, 2), (1, 3), (2, 0), (3, 1)])
    zero_side = jnp.where(z == 0, pair, across)
    one_side = jnp.where(z == 0, across, pair)
    three = jnp.concatenate([zero_side, one_side[:1]])
    got = lax.ppermute(three, "col", [(0, 8), (1, 9), (2, 10), (3, 11)])
    three = jnp.where(z < 2, three, got)
    got = lax.ppermute(
        three, "col", [(c0 + d, c0 + d + 4) for c0 in (0, 8) for d in range(4)]
    )
    three = jnp.where(z % 4 < 2, three, got)
    lead_x = gather(three, "row", X_GROUPS)[:3]
    lead_half = gather(lead_x, "row", Y_GROUPS)
    lead_other = lax.ppermute(lead_half, "col", CORE_SWAP)
    lead = jnp.stack(
        [jnp.where(core == 0, lead_half, lead_other), jnp.where(core == 0, lead_other, lead_half)]
    )
    lead = lead.transpose(2, 1, 0, 4, 3, 5).reshape(LEAD, LEAD)

    columns_x = gather(my_quarter, "row", X_GROUPS)[:3]
    columns = gather(columns_x, "row", Y_GROUPS)
    columns = columns.transpose(1, 2, 0, 3).reshape(LEAD, 4 * TILE)

    def chunk(panel, i):
        return lax.slice_in_dim(panel, 64 * i, 64 * (i + 1))

    arrived = []
    for t in range(1, 8):
        at_zero = jnp.stack([chunk(panel_even, t), chunk(panel_odd, t)])
        one = (t + 1) % 8
        at_one = jnp.stack([chunk(panel_even, one), chunk(panel_odd, one)])
        pairs = [(core0 + 2 * z0, core0 + 2 * ((z0 + t) % 8)) for core0 in range(2) for z0 in range(2)]
        arrived.append(lax.ppermute(jnp.where(z == 0, at_zero, at_one), "col", pairs))
    own_zero = jnp.stack([chunk(panel_even, 0), chunk(panel_odd, 0)])
    own_one = chunk(panel_even, 1)
    from_zero = choose(z, [own_zero] + arrived, 0)
    from_one = choose((z + 7) % 8, [own_one] + [a[0] for a in arrived], 0)
    my_chunk = jnp.concatenate([from_zero, from_one[None]])
    rows_half = gather(my_chunk, "col", Z_GROUPS)
    rows_other = lax.ppermute(rows_half, "col", CORE_SWAP)
    rows = jnp.stack(
        [jnp.where(core == 0, rows_half, rows_other), jnp.where(core == 0, rows_other, rows_half)]
    )
    rows = rows.transpose(0, 1, 3, 2, 4).reshape(4 * TILE, LEAD)

    upper, inverse = factorize(lead)
    panel = dot(rows, inverse, ((1,), (1,)), lax.Precision.HIGHEST)
    across = dot(inverse, columns, ((1,), (0,)), lax.Precision.HIGHEST)
    out = matrix - dot(panel, across, ((1,), (0,)), lax.Precision.HIGHEST)

    at = jnp.minimum(c, 2) * TILE
    solved = lax.dynamic_slice_in_dim(panel, at, TILE, 1)
    out = out.at[:, :TILE].set(jnp.where(c < 3, solved, out[:, :TILE]))
    diagonal = lax.dynamic_slice(upper, (at, jnp.minimum(r, 2) * TILE), (TILE, TILE)).T
    below = jnp.tril(jnp.ones((TILE, TILE), bool))
    corner = jnp.where((c < r) | ((c == r) & below), diagonal, 0.0)
    top = jnp.concatenate([corner, jnp.zeros((TILE, 3 * TILE), jnp.float32)], axis=1)
    return out.at[:TILE].set(jnp.where(r < 3, jnp.where(c < 3, top, 0.0), out[:TILE]))


def solution(mesh):
    placed = (P("row", "col"),)
    return jax.shard_map(
        on_device, mesh=mesh, in_specs=placed, out_specs=P("row", "col"), check_vma=False
    )
```

```python
import jax
import jax.numpy as jnp
from jax import lax
from jax.experimental import pallas as pl
from jax.experimental.pallas import tpu as pltpu
from jax.sharding import PartitionSpec as P

TILE = 256
STEPS = 3
LEAD = TILE * STEPS
BLOCK = 128
SUB = 8
FULL = lax.Precision.HIGHEST

ROW_GROUP = [list(range(16))]
Z_GROUPS = [[2 * z + core for z in range(8)] for core in range(2)]
CORE_SWAP = [(c, c ^ 1) for c in range(16)]
NEAR = [(0, 2), (1, 3), (2, 0), (3, 1)]
EXCHANGE = [(2 * z + k, 2 * (z ^ 1) + k) for z in range(8) for k in range(2) if z % 2 == 0 or k == 0]
FAR = [[(d, d + 4 * i) for d in range(4)] for i in range(4)]
VMEM = pl.BlockSpec(memory_space=pltpu.VMEM)
SMEM = pl.BlockSpec(memory_space=pltpu.SMEM)
NORMAL = ((1,), (0,))
RIGHT_T = ((1,), (1,))
LEFT_T = ((0,), (1,))


def dot(left, right, dims):
    return lax.dot_general(
        left, right, (dims, ((), ())), precision=FULL, preferred_element_type=jnp.float32
    )


def split(value):
    high = value.astype(jnp.bfloat16)
    return high, (value - high.astype(jnp.float32)).astype(jnp.bfloat16)


def spread_lane(value, i):
    return jnp.broadcast_to(value[:, i : i + 1], value.shape)


def factor_block(load, store, shared):
    count = BLOCK // SUB
    sub = lax.broadcasted_iota(jnp.int32, (SUB, BLOCK), 0)
    lane = lax.broadcasted_iota(jnp.int32, (SUB, BLOCK), 1)
    left = [load(k) for k in range(count)]
    right = [(lane == sub + SUB * k).astype(jnp.float32) for k in range(count)]
    for k in range(count):
        for m in range(SUB):
            shared[k % 2, m] = spread_lane(left[k], SUB * k + m)
        shared[k % 2, SUB] = left[k]
        shared[k % 2, SUB + 1] = right[k]
        row = lambda slot, i: jnp.broadcast_to(shared[k % 2, slot, i : i + 1, :], (SUB, BLOCK))
        s = [[None] * SUB for _ in range(SUB)]
        for i in range(SUB):
            for m in range(i, SUB):
                s[i][m] = s[m][i] = row(m, i)
        rows_l = [row(SUB, i) for i in range(SUB)]
        rows_r = [row(SUB + 1, i) for i in range(SUB)]
        out_l, out_r = [None] * SUB, [None] * SUB
        for i in range(0, SUB, 2):
            j = i + 1
            a, b, c = s[i][i], s[i][j], s[j][j]
            det = a * c - b * b
            root_a, root_det = lax.rsqrt(a), lax.rsqrt(det)
            second, inverse = a * root_a * root_det, root_det * root_det
            upper = b * root_a
            out_l[i], out_r[i] = rows_l[i] * root_a, rows_r[i] * root_a
            out_l[j] = (rows_l[j] - upper * out_l[i]) * second
            out_r[j] = (rows_r[j] - upper * out_r[i]) * second
            first_l, second_l = c * rows_l[i] - b * rows_l[j], a * rows_l[j] - b * rows_l[i]
            first_r, second_r = c * rows_r[i] - b * rows_r[j], a * rows_r[j] - b * rows_r[i]
            first, last = [None] * SUB, [None] * SUB
            for n in range(i + 2, SUB):
                first[n], last[n] = c * s[i][n] - b * s[j][n], a * s[j][n] - b * s[i][n]
            for m in range(SUB):
                if m in (i, j):
                    continue
                g, h = s[m][i], s[m][j]
                for n in range(i + 2, SUB):
                    if m > i and n < m:
                        continue
                    s[m][n] = s[m][n] - (g * first[n] + h * last[n]) * inverse
                    if m > i:
                        s[n][m] = s[m][n]
                rows_l[m] = rows_l[m] - (g * first_l + h * second_l) * inverse
                rows_r[m] = rows_r[m] - (g * first_r + h * second_r) * inverse
            for n in range(i + 2, SUB):
                s[i][n], s[j][n] = first[n] * inverse, last[n] * inverse
            rows_l[i], rows_l[j] = first_l * inverse, second_l * inverse
            rows_r[i], rows_r[j] = first_r * inverse, second_r * inverse
        merged_l, merged_r = out_l[0], out_r[0]
        for i in range(1, SUB):
            merged_l = jnp.where(sub == i, out_l[i], merged_l)
            merged_r = jnp.where(sub == i, out_r[i], merged_r)
        store(k, jnp.where(lane >= sub + SUB * k, merged_l, 0.0), merged_r)
        for j in range(k + 1, count):
            weights = [spread_lane(left[j], SUB * k + m) for m in range(SUB)]
            for m in range(SUB):
                left[j] = left[j] - weights[m] * rows_l[m]
                right[j] = right[j] - weights[m] * rows_r[m]


def factor_tile(tile, factor, inverse, upper, lower, shared):
    def block(start):
        def load(k):
            return tile[start + SUB * k : start + SUB * (k + 1), start : start + BLOCK]

        def store(k, rows_u, rows_w):
            upper[SUB * k : SUB * (k + 1), :] = rows_u
            lower[SUB * k : SUB * (k + 1), :] = rows_w

        factor_block(load, store, shared)
        end = start + BLOCK
        factor[start:end, start:end] = upper[...].T
        inverse[start:end, start:end] = lower[...]

    zeros = jnp.zeros((BLOCK, BLOCK), jnp.float32)
    block(0)
    first = lower[...]
    side = dot(tile[BLOCK:, :BLOCK], first, RIGHT_T)
    tile[BLOCK:, BLOCK:] = tile[BLOCK:, BLOCK:] - dot(side, side, RIGHT_T)
    factor[BLOCK:, :BLOCK] = side
    factor[:BLOCK, BLOCK:] = zeros
    inverse[:BLOCK, BLOCK:] = zeros
    block(BLOCK)
    inverse[BLOCK:, :BLOCK] = -dot(lower[...], dot(side, first, NORMAL), NORMAL)


def lead_kernel(where, mine, other, factors, inverses, sides, tiles, upper, lower, shared):
    def place(source, half):
        for y in range(4):
            for x in range(STEPS):
                for w in range(2):
                    start = 64 * y + 32 * half
                    tiles[x, w, start : start + 32, :] = source[4 * y + x, w]

    for core in range(2):

        @pl.when(where[2] == core)
        def _(core=core):
            place(mine, core)
            place(other, 1 - core)

    def step(j, carry):
        factor_tile(tiles.at[j, 0], factors.at[j], inverses.at[j], upper, lower, shared)

        @pl.when(j == 0)
        def _():
            one = dot(tiles[0, 1], inverses[0], LEFT_T)
            tiles[1, 0] = tiles[1, 0] - dot(one, one, RIGHT_T)
            sides[0] = one
            two = dot(tiles[2, 1], inverses[0], RIGHT_T)
            sides[1] = two
            tiles[1, 1] = tiles[1, 1] - dot(one, two, RIGHT_T)
            tiles[2, 0] = tiles[2, 0] - dot(two, two, RIGHT_T)

        @pl.when(j == 1)
        def _():
            two = dot(tiles[1, 1], inverses[1], LEFT_T)
            sides[2] = two
            tiles[2, 0] = tiles[2, 0] - dot(two, two, RIGHT_T)

        return carry

    lax.fori_loop(0, STEPS, step, 0)


def factorize(where, mine, other):
    three = jax.ShapeDtypeStruct((STEPS, TILE, TILE), jnp.float32)
    return pl.pallas_call(
        lead_kernel,
        out_shape=(three, three, three),
        in_specs=[SMEM, VMEM, VMEM],
        out_specs=(VMEM, VMEM, VMEM),
        scratch_shapes=[
            pltpu.VMEM((STEPS, 2, TILE, TILE), jnp.float32),
            pltpu.VMEM((BLOCK, BLOCK), jnp.float32),
            pltpu.VMEM((BLOCK, BLOCK), jnp.float32),
            pltpu.VMEM((2, SUB + 2, SUB, BLOCK), jnp.float32),
        ],
        compiler_params=pltpu.CompilerParams(vmem_limit_bytes=56 * 2**20),
        cost_estimate=pl.CostEstimate(flops=3 * 10**10, bytes_accessed=10**6, transcendentals=0),
    )(where, mine, other)


def update_kernel(
    where, a, mine, other, e, factors, inverses, sides, out, panel, q, q_high, q_low, block
):
    r, c, core = where[0], where[1], where[2]
    t = pl.program_id(0)

    @pl.when(t == 0)
    def _():
        def row(j):
            return jnp.concatenate([e[4 * s + j] for s in range(4)], axis=1)

        q0 = dot(inverses[0], row(0), NORMAL)
        q[...] = q0
        q1 = dot(inverses[1], row(1) - dot(sides[0], q0, NORMAL), NORMAL)
        q_high[:TILE, :], q_low[:TILE, :] = split(q1)
        q2 = row(2) - dot(sides[1], q0, NORMAL) - dot(sides[2], q1, NORMAL)
        q_high[TILE:, :], q_low[TILE:, :] = split(dot(inverses[2], q2, NORMAL))

    def place(lower, upper):
        for i in range(2):
            z, rows = 2 * t + i, 128 * i
            block[rows : rows + 128, :TILE] = lower[z, :128]
            block[rows : rows + 128, TILE : 2 * TILE] = upper[z, :128]
            block[rows : rows + 64, 2 * TILE :] = lower[z, 128:]
            block[rows + 64 : rows + 128, 2 * TILE :] = upper[z, 128:]

    @pl.when(core == 0)
    def _():
        place(mine, other)

    @pl.when(core != 0)
    def _():
        place(other, mine)

    p0 = dot(block[:, :TILE], inverses[0], RIGHT_T)
    p1 = block[:, TILE : 2 * TILE] - dot(p0, sides[0], RIGHT_T)
    p1 = dot(p1, inverses[1], RIGHT_T)
    p2 = block[:, 2 * TILE :] - dot(p0, sides[1], RIGHT_T) - dot(p1, sides[2], RIGHT_T)
    p2 = dot(p2, inverses[2], RIGHT_T)
    panel[:, :TILE] = p0
    panel[:, TILE : 2 * TILE] = p1
    panel[:, 2 * TILE :] = p2
    high, low = split(panel[:, TILE:])
    short = lambda x, y: jnp.dot(x, y, preferred_element_type=jnp.float32)
    qh = q_high[...]
    out[...] = a[...] - (
        dot(p0, q[...], NORMAL) + (short(high, qh) + (short(high, q_low[...]) + short(low, qh)))
    )

    for k in range(STEPS):

        @pl.when(c == k)
        def _(k=k):
            out[:, :TILE] = panel[:, TILE * k : TILE * (k + 1)]

        @pl.when((t == 0) & (r == k))
        def _(k=k):
            out[:, TILE:] = jnp.zeros((TILE, 3 * TILE), jnp.float32)

            @pl.when(c == k)
            def _():
                out[:, :TILE] = factors[k]

            @pl.when(c > k)
            def _():
                out[:, :TILE] = jnp.zeros((TILE, TILE), jnp.float32)


def update(where, matrix, *operands):
    whole = lambda x: pl.BlockSpec(x.shape, lambda t: (0,) * x.ndim)
    row_tile = pl.BlockSpec((TILE, 4 * TILE), lambda t: (t, 0))
    half = pltpu.VMEM((LEAD - TILE, 4 * TILE), jnp.bfloat16)
    return pl.pallas_call(
        update_kernel,
        grid=(4,),
        out_shape=jax.ShapeDtypeStruct(matrix.shape, jnp.float32),
        in_specs=[SMEM, row_tile] + [whole(x) for x in operands],
        out_specs=row_tile,
        scratch_shapes=[
            pltpu.VMEM((TILE, LEAD), jnp.float32),
            pltpu.VMEM((TILE, 4 * TILE), jnp.float32),
            half,
            half,
            pltpu.VMEM((TILE, LEAD), jnp.float32),
        ],
        compiler_params=pltpu.CompilerParams(vmem_limit_bytes=56 * 2**20),
        cost_estimate=pl.CostEstimate(flops=2 * 10**10, bytes_accessed=10**7, transcendentals=0),
    )(where, matrix, *operands)


def after(value, *others):
    return lax.optimization_barrier((value,) + others)[0]


def gather(value, axis, groups):
    copies = jnp.broadcast_to(value[None], (len(groups[0]),) + value.shape)
    return lax.all_to_all(copies, axis, 0, 0, axis_index_groups=groups)


def choose(index, values):
    out = jnp.zeros_like(values[0])
    for i, value in enumerate(values):
        out = jnp.where(index == i, value, out)
    return out


def on_device(matrix):
    r = lax.axis_index("row")
    c = lax.axis_index("col")
    y, x, z, core = r // 4, r % 4, c // 2, c % 2
    where = jnp.stack([r, c, core]).astype(jnp.int32)
    swap = lambda value: lax.ppermute(value, "col", CORE_SWAP)

    def spread(values):
        sent = [lax.ppermute(values[i], "col", FAR[i]) for i in (1, 2, 3)]
        return choose(z // 2, [values[0]] + sent)

    def halves(value):
        size = value.shape[0] // 2
        keep = lax.dynamic_slice_in_dim(value, core * size, size, 0)
        got = swap(lax.dynamic_slice_in_dim(value, (1 - core) * size, size, 0))
        return jnp.stack([jnp.where(core == 0, keep, got), jnp.where(core == 0, got, keep)])

    corner, top, side = matrix[:TILE, :TILE], matrix[:TILE, :], matrix[:, :TILE]
    down = lambda value, s: lax.ppermute(value, "row", [(x0, 4 * s + x0) for x0 in range(3)])

    quarters = [corner[64 * s : 64 * (s + 1)] for s in range(4)]
    quarter = choose(y, [quarters[0]] + [down(quarters[s], s) for s in range(1, 4)])
    pair = halves(quarter)
    across = lax.ppermute(pair, "col", NEAR)
    t0, t1 = jnp.where(z == 0, pair, across)[0], jnp.where(z == 0, pair, across)[1]
    t2 = jnp.where(z == 0, across, pair)[0]
    two = spread([jnp.stack([choose(x, [t0, t1, t2]), choose(x, [t1, t2, t0])])] * 4)

    column = choose(
        y, [top[:, :TILE]] + [down(top[:, TILE * s : TILE * (s + 1)], s) for s in range(1, 4)]
    )

    chunks = side.reshape(4, 2, 128, TILE)
    sent = [chunks[0]] + [lax.ppermute(chunks[i], "col", FAR[i][:3]) for i in (1, 2, 3)]
    two, column, sent = lax.optimization_barrier((two, column, sent))
    e = lax.all_gather(column, "row")
    lead_mine = gather(two, "row", ROW_GROUP)

    couple = choose(z // 2, sent)
    got = lax.ppermute(jnp.where(z % 2 == 0, couple[1], couple[0]), "col", EXCHANGE)
    first = jnp.where(z % 2 == 0, couple[0], got)
    third = jnp.where(z % 2 == 0, got, couple[1])
    got = lax.ppermute(third[64:], "col", [(2 * i, 2 * i + 1) for i in range(8)])
    my_chunk = jnp.concatenate([first, jnp.where(core == 0, third[:64], got)])
    lead_mine, my_chunk = lax.optimization_barrier((lead_mine, my_chunk))
    lead_other = swap(lead_mine)
    rows_mine = gather(my_chunk, "col", Z_GROUPS)
    factors, inverses, sides = factorize(where, lead_mine, lead_other)
    rows_mine, factors = lax.optimization_barrier((rows_mine, factors))
    rows_other = swap(rows_mine)
    return update(where, matrix, rows_mine, rows_other, e, factors, inverses, sides)


def solution(mesh):
    placed = (P("row", "col"),)
    return jax.shard_map(
        on_device, mesh=mesh, in_specs=placed, out_specs=P("row", "col"), check_vma=False
    )
```

```python
import jax
import jax.numpy as jnp
from jax import lax
from jax.experimental import pallas as pl
from jax.experimental.pallas import tpu as pltpu
from jax.sharding import PartitionSpec as P

TILE = 256
STEPS = 3
LEAD = TILE * STEPS
BLOCK = 128
SUB = 8
FULL = lax.Precision.HIGHEST

ROW_GROUP = [list(range(16))]
Z_GROUPS = [[2 * z + core for z in range(8)] for core in range(2)]
CORE_SWAP = [(c, c ^ 1) for c in range(16)]
NEAR = [(0, 2), (1, 3), (2, 0), (3, 1)]
EXCHANGE = [(2 * z + k, 2 * (z ^ 1) + k) for z in range(8) for k in range(2) if z % 2 == 0 or k == 0]
FAR = [[(d, d + 4 * i) for d in range(4)] for i in range(4)]
VMEM = pl.BlockSpec(memory_space=pltpu.VMEM)
SMEM = pl.BlockSpec(memory_space=pltpu.SMEM)
NORMAL = ((1,), (0,))
RIGHT_T = ((1,), (1,))
LEFT_T = ((0,), (1,))


def dot(left, right, dims):
    return lax.dot_general(
        left, right, (dims, ((), ())), precision=FULL, preferred_element_type=jnp.float32
    )


def spread_lane(value, i):
    return jnp.broadcast_to(value[:, i : i + 1], value.shape)


def factor_block(load, store, shared):
    count = BLOCK // SUB
    sub = lax.broadcasted_iota(jnp.int32, (SUB, BLOCK), 0)
    lane = lax.broadcasted_iota(jnp.int32, (SUB, BLOCK), 1)
    left = [load(k) for k in range(count)]
    right = [(lane == sub + SUB * k).astype(jnp.float32) for k in range(count)]
    for k in range(count):
        for m in range(SUB):
            shared[k % 2, m] = spread_lane(left[k], SUB * k + m)
        shared[k % 2, SUB] = left[k]
        shared[k % 2, SUB + 1] = right[k]
        row = lambda slot, i: jnp.broadcast_to(shared[k % 2, slot, i : i + 1, :], (SUB, BLOCK))
        s = [[None] * SUB for _ in range(SUB)]
        for i in range(SUB):
            for m in range(i, SUB):
                s[i][m] = s[m][i] = row(m, i)
        rows_l = [row(SUB, i) for i in range(SUB)]
        rows_r = [row(SUB + 1, i) for i in range(SUB)]
        out_l, out_r = [None] * SUB, [None] * SUB
        for i in range(0, SUB, 2):
            j = i + 1
            a, b, c = s[i][i], s[i][j], s[j][j]
            det = a * c - b * b
            root_a, root_det = lax.rsqrt(a), lax.rsqrt(det)
            second, inverse = a * root_a * root_det, root_det * root_det
            upper = b * root_a
            out_l[i], out_r[i] = rows_l[i] * root_a, rows_r[i] * root_a
            out_l[j] = (rows_l[j] - upper * out_l[i]) * second
            out_r[j] = (rows_r[j] - upper * out_r[i]) * second
            first_l, second_l = c * rows_l[i] - b * rows_l[j], a * rows_l[j] - b * rows_l[i]
            first_r, second_r = c * rows_r[i] - b * rows_r[j], a * rows_r[j] - b * rows_r[i]
            first, last = [None] * SUB, [None] * SUB
            for n in range(i + 2, SUB):
                first[n], last[n] = c * s[i][n] - b * s[j][n], a * s[j][n] - b * s[i][n]
            for m in range(SUB):
                if m in (i, j):
                    continue
                g, h = s[m][i], s[m][j]
                for n in range(i + 2, SUB):
                    if m > i and n < m:
                        continue
                    s[m][n] = s[m][n] - (g * first[n] + h * last[n]) * inverse
                    if m > i:
                        s[n][m] = s[m][n]
                rows_l[m] = rows_l[m] - (g * first_l + h * second_l) * inverse
                rows_r[m] = rows_r[m] - (g * first_r + h * second_r) * inverse
            for n in range(i + 2, SUB):
                s[i][n], s[j][n] = first[n] * inverse, last[n] * inverse
            rows_l[i], rows_l[j] = first_l * inverse, second_l * inverse
            rows_r[i], rows_r[j] = first_r * inverse, second_r * inverse
        merged_l, merged_r = out_l[0], out_r[0]
        for i in range(1, SUB):
            merged_l = jnp.where(sub == i, out_l[i], merged_l)
            merged_r = jnp.where(sub == i, out_r[i], merged_r)
        store(k, jnp.where(lane >= sub + SUB * k, merged_l, 0.0), merged_r)
        for j in range(k + 1, count):
            weights = [spread_lane(left[j], SUB * k + m) for m in range(SUB)]
            for m in range(SUB):
                left[j] = left[j] - weights[m] * rows_l[m]
                right[j] = right[j] - weights[m] * rows_r[m]


def factor_tile(tile, factor, inverse, upper, lower, shared):
    def block(start):
        def load(k):
            return tile[start + SUB * k : start + SUB * (k + 1), start : start + BLOCK]

        def store(k, rows_u, rows_w):
            upper[SUB * k : SUB * (k + 1), :] = rows_u
            lower[SUB * k : SUB * (k + 1), :] = rows_w

        factor_block(load, store, shared)
        end = start + BLOCK
        factor[start:end, start:end] = upper[...].T
        inverse[start:end, start:end] = lower[...]

    zeros = jnp.zeros((BLOCK, BLOCK), jnp.float32)
    block(0)
    first = lower[...]
    side = dot(tile[BLOCK:, :BLOCK], first, RIGHT_T)
    tile[BLOCK:, BLOCK:] = tile[BLOCK:, BLOCK:] - dot(side, side, RIGHT_T)
    factor[BLOCK:, :BLOCK] = side
    factor[:BLOCK, BLOCK:] = zeros
    inverse[:BLOCK, BLOCK:] = zeros
    block(BLOCK)
    inverse[BLOCK:, :BLOCK] = -dot(lower[...], dot(side, first, NORMAL), NORMAL)


def lead_kernel(where, mine, other, factors, inverses, sides, tiles, upper, lower, shared):
    def place(source, half):
        for y in range(4):
            for x in range(STEPS):
                for w in range(2):
                    start = 64 * y + 32 * half
                    tiles[x, w, start : start + 32, :] = source[4 * y + x, w]

    for core in range(2):

        @pl.when(where[2] == core)
        def _(core=core):
            place(mine, core)
            place(other, 1 - core)

    def step(j, carry):
        factor_tile(tiles.at[j, 0], factors.at[j], inverses.at[j], upper, lower, shared)

        @pl.when(j == 0)
        def _():
            one = dot(tiles[0, 1], inverses[0], LEFT_T)
            tiles[1, 0] = tiles[1, 0] - dot(one, one, RIGHT_T)
            sides[0] = one
            two = dot(tiles[2, 1], inverses[0], RIGHT_T)
            sides[1] = two
            tiles[1, 1] = tiles[1, 1] - dot(one, two, RIGHT_T)
            tiles[2, 0] = tiles[2, 0] - dot(two, two, RIGHT_T)

        @pl.when(j == 1)
        def _():
            two = dot(tiles[1, 1], inverses[1], LEFT_T)
            sides[2] = two
            tiles[2, 0] = tiles[2, 0] - dot(two, two, RIGHT_T)

        return carry

    lax.fori_loop(0, STEPS, step, 0)


def factorize(where, mine, other):
    three = jax.ShapeDtypeStruct((STEPS, TILE, TILE), jnp.float32)
    return pl.pallas_call(
        lead_kernel,
        out_shape=(three, three, three),
        in_specs=[SMEM, VMEM, VMEM],
        out_specs=(VMEM, VMEM, VMEM),
        scratch_shapes=[
            pltpu.VMEM((STEPS, 2, TILE, TILE), jnp.float32),
            pltpu.VMEM((BLOCK, BLOCK), jnp.float32),
            pltpu.VMEM((BLOCK, BLOCK), jnp.float32),
            pltpu.VMEM((2, SUB + 2, SUB, BLOCK), jnp.float32),
        ],
        compiler_params=pltpu.CompilerParams(vmem_limit_bytes=56 * 2**20),
        cost_estimate=pl.CostEstimate(flops=3 * 10**10, bytes_accessed=10**6, transcendentals=0),
    )(where, mine, other)


def parts(value, count):
    out = []
    for _ in range(count):
        out.append(value.astype(jnp.bfloat16))
        value = value - out[-1].astype(jnp.float32)
    return out


def stack(ref, value, count):
    size = value.shape[0]
    for i, part in enumerate(parts(value, count)):
        start = size * (count - 1 - i)
        ref[start : start + size, :] = part


def times(value, ref, count):
    size = value.shape[1]
    total = None
    for i, part in reversed(list(enumerate(parts(value, count)))):
        left = jnp.concatenate([part] * (count - i), axis=1)
        product = jnp.dot(left, ref[size * i :, :], preferred_element_type=jnp.float32)
        total = product if total is None else total + product
    return total


def across_kernel(e, inverses, sides, q):
    def row(j):
        return jnp.concatenate([e[4 * s + j] for s in range(4)], axis=1)

    q0 = dot(inverses[0], row(0), NORMAL)
    stack(q.at[:LEAD], q0, 3)
    q1 = dot(inverses[1], row(1) - dot(sides[0], q0, NORMAL), NORMAL)
    q2 = row(2) - dot(sides[1], q0, NORMAL) - dot(sides[2], q1, NORMAL)
    q2 = dot(inverses[2], q2, NORMAL)
    for i, value in enumerate((q1, q2)):
        high, low = parts(value, 2)
        start = LEAD + TILE * i
        q[start : start + TILE, :] = high
        q[start + 2 * TILE : start + 3 * TILE, :] = low


def across(e, inverses, sides):
    return pl.pallas_call(
        across_kernel,
        out_shape=jax.ShapeDtypeStruct((7 * TILE, 4 * TILE), jnp.bfloat16),
        in_specs=[VMEM] * 3,
        out_specs=VMEM,
        compiler_params=pltpu.CompilerParams(vmem_limit_bytes=56 * 2**20),
        cost_estimate=pl.CostEstimate(flops=10**10, bytes_accessed=10**7, transcendentals=0),
    )(e, inverses, sides)


def update_kernel(
    where, a, mine, other, q, factors, inverses, sides, out, panel, block, right0, right1, rights
):
    r, c, core = where[0], where[1], where[2]
    t = pl.program_id(0)

    @pl.when(t == 0)
    def _():
        stack(right0, inverses[0].T, 3)
        stack(right1, jnp.concatenate([sides[0].T, sides[1].T], axis=1), 3)
        for i, value in enumerate((inverses[1], sides[2], inverses[2])):
            stack(rights.at[i], value.T, 2)

    def place(lower, upper):
        for i in range(2):
            z, rows = 2 * t + i, 128 * i
            block[rows : rows + 128, :TILE] = lower[z, :128]
            block[rows : rows + 128, TILE : 2 * TILE] = upper[z, :128]
            block[rows : rows + 64, 2 * TILE :] = lower[z, 128:]
            block[rows + 64 : rows + 128, 2 * TILE :] = upper[z, 128:]

    @pl.when(core == 0)
    def _():
        place(mine, other)

    @pl.when(core != 0)
    def _():
        place(other, mine)

    p0 = times(block[:, :TILE], right0, 3)
    removed = times(p0, right1, 3)
    p1 = times(block[:, TILE : 2 * TILE] - removed[:, :TILE], rights.at[0], 2)
    p2 = block[:, 2 * TILE :] - removed[:, TILE:] - times(p1, rights.at[1], 2)
    p2 = times(p2, rights.at[2], 2)
    panel[:, :TILE] = p0
    panel[:, TILE : 2 * TILE] = p1
    panel[:, 2 * TILE :] = p2

    first, second, third = parts(p0, 3)
    high, low = parts(panel[:, TILE:], 2)
    short = lambda x, y: jnp.dot(x, y, preferred_element_type=jnp.float32)
    total = short(third, q[2 * TILE : 3 * TILE, :])
    total = total + short(jnp.concatenate([second, second, low], axis=1), q[TILE : 5 * TILE, :])
    total = total + short(jnp.concatenate([first, first, first, high, high], axis=1), q[...])
    out[...] = a[...] - total

    for k in range(STEPS):

        @pl.when(c == k)
        def _(k=k):
            out[:, :TILE] = panel[:, TILE * k : TILE * (k + 1)]

        @pl.when((t == 0) & (r == k))
        def _(k=k):
            out[:, TILE:] = jnp.zeros((TILE, 3 * TILE), jnp.float32)

            @pl.when(c == k)
            def _():
                out[:, :TILE] = factors[k]

            @pl.when(c > k)
            def _():
                out[:, :TILE] = jnp.zeros((TILE, TILE), jnp.float32)


def update(where, matrix, *operands):
    whole = lambda x: pl.BlockSpec(x.shape, lambda t: (0,) * x.ndim)
    row_tile = pl.BlockSpec((TILE, 4 * TILE), lambda t: (t, 0))
    return pl.pallas_call(
        update_kernel,
        grid=(4,),
        out_shape=jax.ShapeDtypeStruct(matrix.shape, jnp.float32),
        in_specs=[SMEM, row_tile] + [whole(x) for x in operands],
        out_specs=row_tile,
        scratch_shapes=[
            pltpu.VMEM((TILE, LEAD), jnp.float32),
            pltpu.VMEM((TILE, LEAD), jnp.float32),
            pltpu.VMEM((3 * TILE, TILE), jnp.bfloat16),
            pltpu.VMEM((3 * TILE, 2 * TILE), jnp.bfloat16),
            pltpu.VMEM((STEPS, 2 * TILE, TILE), jnp.bfloat16),
        ],
        compiler_params=pltpu.CompilerParams(vmem_limit_bytes=56 * 2**20),
        cost_estimate=pl.CostEstimate(flops=2 * 10**10, bytes_accessed=10**7, transcendentals=0),
    )(where, matrix, *operands)


def after(value, *others):
    return lax.optimization_barrier((value,) + others)[0]


def gather(value, axis, groups):
    copies = jnp.broadcast_to(value[None], (len(groups[0]),) + value.shape)
    return lax.all_to_all(copies, axis, 0, 0, axis_index_groups=groups)


def choose(index, values):
    out = jnp.zeros_like(values[0])
    for i, value in enumerate(values):
        out = jnp.where(index == i, value, out)
    return out


def on_device(matrix):
    r = lax.axis_index("row")
    c = lax.axis_index("col")
    y, x, z, core = r // 4, r % 4, c // 2, c % 2
    where = jnp.stack([r, c, core]).astype(jnp.int32)
    swap = lambda value: lax.ppermute(value, "col", CORE_SWAP)

    def spread(values):
        sent = [lax.ppermute(values[i], "col", FAR[i]) for i in (1, 2, 3)]
        return choose(z // 2, [values[0]] + sent)

    def halves(value):
        size = value.shape[0] // 2
        keep = lax.dynamic_slice_in_dim(value, core * size, size, 0)
        got = swap(lax.dynamic_slice_in_dim(value, (1 - core) * size, size, 0))
        return jnp.stack([jnp.where(core == 0, keep, got), jnp.where(core == 0, got, keep)])

    corner, top, side = matrix[:TILE, :TILE], matrix[:TILE, :], matrix[:, :TILE]
    down = lambda value, s: lax.ppermute(value, "row", [(x0, 4 * s + x0) for x0 in range(3)])

    quarters = [corner[64 * s : 64 * (s + 1)] for s in range(4)]
    quarter = choose(y, [quarters[0]] + [down(quarters[s], s) for s in range(1, 4)])
    pair = halves(quarter)
    next_door = lax.ppermute(pair, "col", NEAR)
    t0, t1 = jnp.where(z == 0, pair, next_door)[0], jnp.where(z == 0, pair, next_door)[1]
    t2 = jnp.where(z == 0, next_door, pair)[0]
    two = spread([jnp.stack([choose(x, [t0, t1, t2]), choose(x, [t1, t2, t0])])] * 4)

    column = choose(
        y, [top[:, :TILE]] + [down(top[:, TILE * s : TILE * (s + 1)], s) for s in range(1, 4)]
    )

    chunks = after(side, two).reshape(4, 2, 128, TILE)
    sent = [chunks[0]] + [lax.ppermute(chunks[i], "col", FAR[i][:3]) for i in (1, 2, 3)]
    two, column = lax.optimization_barrier((two, column))
    e = lax.all_gather(column, "row")
    lead_mine = gather(two, "row", ROW_GROUP)

    couple = choose(z // 2, sent)
    got = lax.ppermute(jnp.where(z % 2 == 0, couple[1], couple[0]), "col", EXCHANGE)
    first = jnp.where(z % 2 == 0, couple[0], got)
    third = jnp.where(z % 2 == 0, got, couple[1])
    got = lax.ppermute(third[64:], "col", [(2 * i, 2 * i + 1) for i in range(8)])
    my_chunk = jnp.concatenate([first, jnp.where(core == 0, third[:64], got)])
    lead_mine, my_chunk = lax.optimization_barrier((lead_mine, my_chunk))
    lead_other = swap(lead_mine)
    rows_mine = gather(my_chunk, "col", Z_GROUPS)
    factors, inverses, sides = factorize(where, lead_mine, lead_other)
    q = across(e, inverses, sides)
    rows_mine, q = lax.optimization_barrier((rows_mine, q))
    rows_other = swap(rows_mine)
    return update(where, matrix, rows_mine, rows_other, q, factors, inverses, sides)


def solution(mesh):
    placed = (P("row", "col"),)
    return jax.shard_map(
        on_device, mesh=mesh, in_specs=placed, out_specs=P("row", "col"), check_vma=False
    )
```

```python
import jax
import jax.numpy as jnp
from jax import lax
from jax.experimental import pallas as pl
from jax.experimental.pallas import tpu as pltpu
from jax.sharding import PartitionSpec as P

TILE = 256
STEPS = 3
LEAD = TILE * STEPS
BLOCK = 128
SUB = 8
FULL = lax.Precision.HIGHEST

ROW_GROUP = [list(range(16))]
Z_GROUPS = [[2 * z + core for z in range(8)] for core in range(2)]
CORE_SWAP = [(c, c ^ 1) for c in range(16)]
NEAR = [(0, 2), (1, 3), (2, 0), (3, 1)]
EXCHANGE = [(2 * z + k, 2 * (z ^ 1) + k) for z in range(8) for k in range(2) if z % 2 == 0 or k == 0]
FAR = [[(d, d + 4 * i) for d in range(4)] for i in range(4)]
VMEM = pl.BlockSpec(memory_space=pltpu.VMEM)
SMEM = pl.BlockSpec(memory_space=pltpu.SMEM)
NORMAL = ((1,), (0,))
RIGHT_T = ((1,), (1,))
LEFT_T = ((0,), (1,))


def dot(left, right, dims):
    return lax.dot_general(
        left, right, (dims, ((), ())), precision=FULL, preferred_element_type=jnp.float32
    )


def spread_lane(value, i):
    return jnp.broadcast_to(value[:, i : i + 1], value.shape)


def factor_block(load, store, shared):
    count = BLOCK // SUB
    sub = lax.broadcasted_iota(jnp.int32, (SUB, BLOCK), 0)
    lane = lax.broadcasted_iota(jnp.int32, (SUB, BLOCK), 1)
    left = [load(k) for k in range(count)]
    right = [(lane == sub + SUB * k).astype(jnp.float32) for k in range(count)]
    for k in range(count):
        for m in range(SUB):
            shared[k % 2, m] = spread_lane(left[k], SUB * k + m)
        shared[k % 2, SUB] = left[k]
        shared[k % 2, SUB + 1] = right[k]
        row = lambda slot, i: jnp.broadcast_to(shared[k % 2, slot, i : i + 1, :], (SUB, BLOCK))
        s = [[None] * SUB for _ in range(SUB)]
        for i in range(SUB):
            for m in range(i, SUB):
                s[i][m] = s[m][i] = row(m, i)
        rows_l = [row(SUB, i) for i in range(SUB)]
        rows_r = [row(SUB + 1, i) for i in range(SUB)]
        out_l, out_r = [None] * SUB, [None] * SUB
        for i in range(0, SUB, 2):
            j = i + 1
            a, b, c = s[i][i], s[i][j], s[j][j]
            det = a * c - b * b
            root_a, root_det = lax.rsqrt(a), lax.rsqrt(det)
            second, inverse = a * root_a * root_det, root_det * root_det
            upper = b * root_a
            out_l[i], out_r[i] = rows_l[i] * root_a, rows_r[i] * root_a
            out_l[j] = (rows_l[j] - upper * out_l[i]) * second
            out_r[j] = (rows_r[j] - upper * out_r[i]) * second
            first_l, second_l = c * rows_l[i] - b * rows_l[j], a * rows_l[j] - b * rows_l[i]
            first_r, second_r = c * rows_r[i] - b * rows_r[j], a * rows_r[j] - b * rows_r[i]
            first, last = [None] * SUB, [None] * SUB
            for n in range(i + 2, SUB):
                first[n], last[n] = c * s[i][n] - b * s[j][n], a * s[j][n] - b * s[i][n]
            for m in range(SUB):
                if m in (i, j):
                    continue
                g, h = s[m][i], s[m][j]
                for n in range(i + 2, SUB):
                    if m > i and n < m:
                        continue
                    s[m][n] = s[m][n] - (g * first[n] + h * last[n]) * inverse
                    if m > i:
                        s[n][m] = s[m][n]
                rows_l[m] = rows_l[m] - (g * first_l + h * second_l) * inverse
                rows_r[m] = rows_r[m] - (g * first_r + h * second_r) * inverse
            for n in range(i + 2, SUB):
                s[i][n], s[j][n] = first[n] * inverse, last[n] * inverse
            rows_l[i], rows_l[j] = first_l * inverse, second_l * inverse
            rows_r[i], rows_r[j] = first_r * inverse, second_r * inverse
        merged_l, merged_r = out_l[0], out_r[0]
        for i in range(1, SUB):
            merged_l = jnp.where(sub == i, out_l[i], merged_l)
            merged_r = jnp.where(sub == i, out_r[i], merged_r)
        store(k, jnp.where(lane >= sub + SUB * k, merged_l, 0.0), merged_r)
        for j in range(k + 1, count):
            weights = [spread_lane(left[j], SUB * k + m) for m in range(SUB)]
            for m in range(SUB):
                left[j] = left[j] - weights[m] * rows_l[m]
                right[j] = right[j] - weights[m] * rows_r[m]


def factor_tile(tile, factor, inverse, upper, lower, shared):
    def block(start):
        def load(k):
            return tile[start + SUB * k : start + SUB * (k + 1), start : start + BLOCK]

        def store(k, rows_u, rows_w):
            upper[SUB * k : SUB * (k + 1), :] = rows_u
            lower[SUB * k : SUB * (k + 1), :] = rows_w

        factor_block(load, store, shared)
        end = start + BLOCK
        factor[start:end, start:end] = upper[...].T
        inverse[start:end, start:end] = lower[...]

    zeros = jnp.zeros((BLOCK, BLOCK), jnp.float32)
    block(0)
    first = lower[...]
    side = dot(tile[BLOCK:, :BLOCK], first, RIGHT_T)
    tile[BLOCK:, BLOCK:] = tile[BLOCK:, BLOCK:] - dot(side, side, RIGHT_T)
    factor[BLOCK:, :BLOCK] = side
    factor[:BLOCK, BLOCK:] = zeros
    inverse[:BLOCK, BLOCK:] = zeros
    block(BLOCK)
    inverse[BLOCK:, :BLOCK] = -dot(lower[...], dot(side, first, NORMAL), NORMAL)


def lead_kernel(where, mine, other, factors, inverses, sides, tiles, upper, lower, shared):
    def place(source, half):
        for y in range(4):
            for x in range(STEPS):
                for w in range(2):
                    start = 64 * y + 32 * half
                    tiles[x, w, start : start + 32, :] = source[4 * y + x, w]

    for core in range(2):

        @pl.when(where[2] == core)
        def _(core=core):
            place(mine, core)
            place(other, 1 - core)

    def step(j, carry):
        factor_tile(tiles.at[j, 0], factors.at[j], inverses.at[j], upper, lower, shared)

        @pl.when(j == 0)
        def _():
            one = dot(tiles[0, 1], inverses[0], LEFT_T)
            tiles[1, 0] = tiles[1, 0] - dot(one, one, RIGHT_T)
            sides[0] = one
            two = dot(tiles[2, 1], inverses[0], RIGHT_T)
            sides[1] = two
            tiles[1, 1] = tiles[1, 1] - dot(one, two, RIGHT_T)
            tiles[2, 0] = tiles[2, 0] - dot(two, two, RIGHT_T)

        @pl.when(j == 1)
        def _():
            two = dot(tiles[1, 1], inverses[1], LEFT_T)
            sides[2] = two
            tiles[2, 0] = tiles[2, 0] - dot(two, two, RIGHT_T)

        return carry

    lax.fori_loop(0, STEPS, step, 0)


def factorize(where, mine, other):
    three = jax.ShapeDtypeStruct((STEPS, TILE, TILE), jnp.float32)
    return pl.pallas_call(
        lead_kernel,
        out_shape=(three, three, three),
        in_specs=[SMEM, VMEM, VMEM],
        out_specs=(VMEM, VMEM, VMEM),
        scratch_shapes=[
            pltpu.VMEM((STEPS, 2, TILE, TILE), jnp.float32),
            pltpu.VMEM((BLOCK, BLOCK), jnp.float32),
            pltpu.VMEM((BLOCK, BLOCK), jnp.float32),
            pltpu.VMEM((2, SUB + 2, SUB, BLOCK), jnp.float32),
        ],
        compiler_params=pltpu.CompilerParams(vmem_limit_bytes=56 * 2**20),
        cost_estimate=pl.CostEstimate(flops=3 * 10**10, bytes_accessed=10**6, transcendentals=0),
    )(where, mine, other)


def parts(value, count):
    out = []
    for _ in range(count):
        out.append(value.astype(jnp.bfloat16))
        value = value - out[-1].astype(jnp.float32)
    return out


def stack(ref, value, count):
    size = value.shape[0]
    for i, part in enumerate(parts(value, count)):
        start = size * (count - 1 - i)
        ref[start : start + size, :] = part


def times(value, ref, count):
    size = value.shape[1]
    total = None
    for i, part in reversed(list(enumerate(parts(value, count)))):
        left = jnp.concatenate([part] * (count - i), axis=1)
        product = jnp.dot(left, ref[size * i :, :], preferred_element_type=jnp.float32)
        total = product if total is None else total + product
    return total


def across_kernel(e, inverses, sides, q):
    def row(j):
        return jnp.concatenate([e[4 * s + j] for s in range(4)], axis=1)

    q0 = dot(inverses[0], row(0), NORMAL)
    stack(q.at[:LEAD], q0, 3)
    q1 = dot(inverses[1], row(1) - dot(sides[0], q0, NORMAL), NORMAL)
    q2 = row(2) - dot(sides[1], q0, NORMAL) - dot(sides[2], q1, NORMAL)
    q2 = dot(inverses[2], q2, NORMAL)
    for i, value in enumerate((q1, q2)):
        high, low = parts(value, 2)
        start = LEAD + TILE * i
        q[start : start + TILE, :] = high
        q[start + 2 * TILE : start + 3 * TILE, :] = low


def across(e, inverses, sides):
    return pl.pallas_call(
        across_kernel,
        out_shape=jax.ShapeDtypeStruct((7 * TILE, 4 * TILE), jnp.bfloat16),
        in_specs=[VMEM] * 3,
        out_specs=VMEM,
        compiler_params=pltpu.CompilerParams(vmem_limit_bytes=56 * 2**20),
        cost_estimate=pl.CostEstimate(flops=10**10, bytes_accessed=10**7, transcendentals=0),
    )(e, inverses, sides)


def update_kernel(
    where, a, mine, other, q_far, factors, inverses, sides, out,
    panel_all, block, right0, right1, rights, q, arrival
):
    r, c, core = where[0], where[1], where[2]
    t = pl.program_id(0)

    fetch = pltpu.make_async_copy(q_far, q, arrival)

    @pl.when(t == 0)
    def _():
        fetch.start()
        stack(right0, inverses[0].T, 3)
        stack(right1, jnp.concatenate([sides[0].T, sides[1].T], axis=1), 3)
        for i, value in enumerate((inverses[1], sides[2], inverses[2])):
            stack(rights.at[i], value.T, 2)

    def place(lower, upper):
        for z in range(8):
            rows = 128 * z
            block[rows : rows + 128, :TILE] = lower[z, :128]
            block[rows : rows + 128, TILE : 2 * TILE] = upper[z, :128]
            block[rows : rows + 64, 2 * TILE :] = lower[z, 128:]
            block[rows + 64 : rows + 128, 2 * TILE :] = upper[z, 128:]

    @pl.when((t == 0) & (core == 0))
    def _():
        place(mine, other)

    @pl.when((t == 0) & (core != 0))
    def _():
        place(other, mine)

    @pl.when(t == 0)
    def _():
        p0 = times(block[:, :TILE], right0, 3)
        panel_all[:, :TILE] = p0
        removed = times(p0, right1, 3)
        p1 = times(block[:, TILE : 2 * TILE] - removed[:, :TILE], rights.at[0], 2)
        panel_all[:, TILE : 2 * TILE] = p1
        p2 = block[:, 2 * TILE :] - removed[:, TILE:] - times(p1, rights.at[1], 2)
        panel_all[:, 2 * TILE :] = times(p2, rights.at[2], 2)
        fetch.wait()

    panel = panel_all.at[pl.ds(pl.multiple_of(t * TILE, TILE), TILE)]
    p0 = panel[:, :TILE]

    first, second, third = parts(p0, 3)
    high, low = parts(panel[:, TILE:], 2)
    short = lambda x, y: jnp.dot(x, y, preferred_element_type=jnp.float32)
    total = short(third, q[2 * TILE : 3 * TILE, :])
    total = total + short(jnp.concatenate([second, second, low], axis=1), q[TILE : 5 * TILE, :])
    total = total + short(jnp.concatenate([first, first, first, high, high], axis=1), q[...])
    out[...] = a[...] - total

    for k in range(STEPS):

        @pl.when(c == k)
        def _(k=k):
            out[:, :TILE] = panel[:, TILE * k : TILE * (k + 1)]

        @pl.when((t == 0) & (r == k))
        def _(k=k):
            out[:, TILE:] = jnp.zeros((TILE, 3 * TILE), jnp.float32)

            @pl.when(c == k)
            def _():
                out[:, :TILE] = factors[k]

            @pl.when(c > k)
            def _():
                out[:, :TILE] = jnp.zeros((TILE, TILE), jnp.float32)


def update(where, matrix, *operands):
    whole = lambda x: pl.BlockSpec(x.shape, lambda t: (0,) * x.ndim)
    row_tile = pl.BlockSpec((TILE, 4 * TILE), lambda t: (t, 0))
    return pl.pallas_call(
        update_kernel,
        grid=(4,),
        out_shape=jax.ShapeDtypeStruct(matrix.shape, jnp.float32),
        in_specs=[SMEM, row_tile] + [whole(x) for x in operands[:2]]
        + [pl.BlockSpec(memory_space=pl.ANY)]
        + [whole(x) for x in operands[3:]],
        out_specs=row_tile,
        scratch_shapes=[
            pltpu.VMEM((4 * TILE, LEAD), jnp.float32),
            pltpu.VMEM((4 * TILE, LEAD), jnp.float32),
            pltpu.VMEM((3 * TILE, TILE), jnp.bfloat16),
            pltpu.VMEM((3 * TILE, 2 * TILE), jnp.bfloat16),
            pltpu.VMEM((STEPS, 2 * TILE, TILE), jnp.bfloat16),
            pltpu.VMEM((7 * TILE, 4 * TILE), jnp.bfloat16),
            pltpu.SemaphoreType.DMA,
        ],
        compiler_params=pltpu.CompilerParams(vmem_limit_bytes=56 * 2**20),
        cost_estimate=pl.CostEstimate(flops=2 * 10**10, bytes_accessed=10**7, transcendentals=0),
    )(where, matrix, *operands)


def after(value, *others):
    return lax.optimization_barrier((value,) + others)[0]


def copies(value, groups):
    return jnp.broadcast_to(value[None], (len(groups[0]),) + value.shape)


def gather(copied, axis, groups):
    return lax.all_to_all(copied, axis, 0, 0, axis_index_groups=groups)


def choose(index, values):
    out = jnp.zeros_like(values[0])
    for i, value in enumerate(values):
        out = jnp.where(index == i, value, out)
    return out


def on_device(matrix):
    r = lax.axis_index("row")
    c = lax.axis_index("col")
    y, x, z, core = r // 4, r % 4, c // 2, c % 2
    where = jnp.stack([r, c, core]).astype(jnp.int32)
    swap = lambda value: lax.ppermute(value, "col", CORE_SWAP)

    def spread(values):
        sent = [lax.ppermute(values[i], "col", FAR[i]) for i in (1, 2, 3)]
        return choose(z // 2, [values[0]] + sent)

    def halves(value):
        size = value.shape[0] // 2
        keep = lax.dynamic_slice_in_dim(value, core * size, size, 0)
        got = swap(lax.dynamic_slice_in_dim(value, (1 - core) * size, size, 0))
        return jnp.stack([jnp.where(core == 0, keep, got), jnp.where(core == 0, got, keep)])

    corner, top, side = matrix[:TILE, :TILE], matrix[:TILE, :], matrix[:, :TILE]
    down = lambda value, s: lax.ppermute(value, "row", [(x0, 4 * s + x0) for x0 in range(3)])

    quarters = [corner[64 * s : 64 * (s + 1)] for s in range(4)]
    quarter = choose(y, [quarters[0]] + [down(quarters[s], s) for s in range(1, 4)])
    pair = halves(quarter)
    next_door = lax.ppermute(pair, "col", NEAR)
    t0, t1 = jnp.where(z == 0, pair, next_door)[0], jnp.where(z == 0, pair, next_door)[1]
    t2 = jnp.where(z == 0, next_door, pair)[0]
    two = spread([jnp.stack([choose(x, [t0, t1, t2]), choose(x, [t1, t2, t0])])] * 4)

    column = choose(
        y, [top[:, :TILE]] + [down(top[:, TILE * s : TILE * (s + 1)], s) for s in range(1, 4)]
    )

    chunks = after(side, two).reshape(4, 2, 128, TILE)
    sent = [chunks[0]] + [lax.ppermute(chunks[i], "col", FAR[i][:3]) for i in (1, 2, 3)]
    two, column = lax.optimization_barrier((two, column))
    e = lax.all_gather(column, "row")
    lead_mine = gather(copies(two, ROW_GROUP), "row", ROW_GROUP)

    couple = choose(z // 2, sent)
    got = lax.ppermute(jnp.where(z % 2 == 0, couple[1], couple[0]), "col", EXCHANGE)
    first = jnp.where(z % 2 == 0, couple[0], got)
    third = jnp.where(z % 2 == 0, got, couple[1])
    got = lax.ppermute(third[64:], "col", [(2 * i, 2 * i + 1) for i in range(8)])
    my_chunk = jnp.concatenate([first, jnp.where(core == 0, third[:64], got)])
    chunk_copies = copies(my_chunk, Z_GROUPS)
    lead_mine, chunk_copies = lax.optimization_barrier((lead_mine, chunk_copies))
    lead_other = swap(lead_mine)
    rows_mine = gather(chunk_copies, "col", Z_GROUPS)
    factors, inverses, sides = factorize(where, lead_mine, lead_other)
    q = across(e, inverses, sides)
    rows_mine, q = lax.optimization_barrier((rows_mine, q))
    rows_other = swap(rows_mine)
    return update(where, matrix, rows_mine, rows_other, q, factors, inverses, sides)


def solution(mesh):
    placed = (P("row", "col"),)
    return jax.shard_map(
        on_device, mesh=mesh, in_specs=placed, out_specs=P("row", "col"), check_vma=False
    )
```

```python
import jax
import jax.numpy as jnp
from jax import lax
from jax.experimental import pallas as pl
from jax.experimental.pallas import tpu as pltpu
from jax.sharding import PartitionSpec as P

TILE = 256
STEPS = 3
LEAD = TILE * STEPS
BLOCK = 128
SUB = 8
FULL = lax.Precision.HIGHEST

ROW_GROUP = [list(range(16))]
Z_GROUPS = [[2 * z + core for z in range(8)] for core in range(2)]
CORE_SWAP = [(c, c ^ 1) for c in range(16)]
NEAR = [(0, 2), (1, 3), (2, 0), (3, 1)]
EXCHANGE = [(2 * z + k, 2 * (z ^ 1) + k) for z in range(8) for k in range(2) if z % 2 == 0 or k == 0]
FAR = [[(d, d + 4 * i) for d in range(4)] for i in range(4)]
VMEM = pl.BlockSpec(memory_space=pltpu.VMEM)
SMEM = pl.BlockSpec(memory_space=pltpu.SMEM)
NORMAL = ((1,), (0,))
RIGHT_T = ((1,), (1,))
LEFT_T = ((0,), (1,))


def dot(left, right, dims):
    return lax.dot_general(
        left, right, (dims, ((), ())), precision=FULL, preferred_element_type=jnp.float32
    )


def spread_lane(value, i):
    return jnp.broadcast_to(value[:, i : i + 1], value.shape)


def factor_block(load, store, shared):
    count = BLOCK // SUB
    sub = lax.broadcasted_iota(jnp.int32, (SUB, BLOCK), 0)
    lane = lax.broadcasted_iota(jnp.int32, (SUB, BLOCK), 1)
    left = [load(k) for k in range(count)]
    right = [(lane == sub + SUB * k).astype(jnp.float32) for k in range(count)]
    for k in range(count):
        for m in range(SUB):
            shared[k % 2, m] = spread_lane(left[k], SUB * k + m)
        shared[k % 2, SUB] = left[k]
        shared[k % 2, SUB + 1] = right[k]
        row = lambda slot, i: jnp.broadcast_to(shared[k % 2, slot, i : i + 1, :], (SUB, BLOCK))
        s = [[None] * SUB for _ in range(SUB)]
        for i in range(SUB):
            for m in range(i, SUB):
                s[i][m] = s[m][i] = row(m, i)
        rows_l = [row(SUB, i) for i in range(SUB)]
        rows_r = [row(SUB + 1, i) for i in range(SUB)]
        out_l, out_r = [None] * SUB, [None] * SUB
        for i in range(0, SUB, 2):
            j = i + 1
            a, b, c = s[i][i], s[i][j], s[j][j]
            det = a * c - b * b
            root_a, root_det = lax.rsqrt(a), lax.rsqrt(det)
            second, inverse = a * root_a * root_det, root_det * root_det
            upper = b * root_a
            out_l[i], out_r[i] = rows_l[i] * root_a, rows_r[i] * root_a
            out_l[j] = (rows_l[j] - upper * out_l[i]) * second
            out_r[j] = (rows_r[j] - upper * out_r[i]) * second
            first_l, second_l = c * rows_l[i] - b * rows_l[j], a * rows_l[j] - b * rows_l[i]
            first_r, second_r = c * rows_r[i] - b * rows_r[j], a * rows_r[j] - b * rows_r[i]
            first, last = [None] * SUB, [None] * SUB
            for n in range(i + 2, SUB):
                first[n], last[n] = c * s[i][n] - b * s[j][n], a * s[j][n] - b * s[i][n]
            for m in range(SUB):
                if m in (i, j):
                    continue
                g, h = s[m][i], s[m][j]
                for n in range(i + 2, SUB):
                    if m > i and n < m:
                        continue
                    s[m][n] = s[m][n] - (g * first[n] + h * last[n]) * inverse
                    if m > i:
                        s[n][m] = s[m][n]
                rows_l[m] = rows_l[m] - (g * first_l + h * second_l) * inverse
                rows_r[m] = rows_r[m] - (g * first_r + h * second_r) * inverse
            for n in range(i + 2, SUB):
                s[i][n], s[j][n] = first[n] * inverse, last[n] * inverse
            rows_l[i], rows_l[j] = first_l * inverse, second_l * inverse
            rows_r[i], rows_r[j] = first_r * inverse, second_r * inverse
        merged_l, merged_r = out_l[0], out_r[0]
        for i in range(1, SUB):
            merged_l = jnp.where(sub == i, out_l[i], merged_l)
            merged_r = jnp.where(sub == i, out_r[i], merged_r)
        store(k, jnp.where(lane >= sub + SUB * k, merged_l, 0.0), merged_r)
        for j in range(k + 1, count):
            weights = [spread_lane(left[j], SUB * k + m) for m in range(SUB)]
            for m in range(SUB):
                left[j] = left[j] - weights[m] * rows_l[m]
                right[j] = right[j] - weights[m] * rows_r[m]


def factor_tile(tile, factor, inverse, upper, lower, shared):
    def block(start):
        def load(k):
            return tile[start + SUB * k : start + SUB * (k + 1), start : start + BLOCK]

        def store(k, rows_u, rows_w):
            upper[SUB * k : SUB * (k + 1), :] = rows_u
            lower[SUB * k : SUB * (k + 1), :] = rows_w

        factor_block(load, store, shared)
        end = start + BLOCK
        factor[start:end, start:end] = upper[...].T
        inverse[start:end, start:end] = lower[...]

    zeros = jnp.zeros((BLOCK, BLOCK), jnp.float32)
    block(0)
    first = lower[...]
    side = dot(tile[BLOCK:, :BLOCK], first, RIGHT_T)
    tile[BLOCK:, BLOCK:] = tile[BLOCK:, BLOCK:] - dot(side, side, RIGHT_T)
    factor[BLOCK:, :BLOCK] = side
    factor[:BLOCK, BLOCK:] = zeros
    inverse[:BLOCK, BLOCK:] = zeros
    block(BLOCK)
    inverse[BLOCK:, :BLOCK] = -dot(lower[...], dot(side, first, NORMAL), NORMAL)


def lead_kernel(where, mine, other, factors, inverses, sides, tiles, upper, lower, shared):
    def place(source, half):
        for y in range(4):
            for x in range(STEPS):
                for w in range(2):
                    start = 64 * y + 32 * half
                    tiles[x, w, start : start + 32, :] = source[4 * y + x, w]

    for core in range(2):

        @pl.when(where[2] == core)
        def _(core=core):
            place(mine, core)
            place(other, 1 - core)

    def step(j, carry):
        factor_tile(tiles.at[j, 0], factors.at[j], inverses.at[j], upper, lower, shared)

        @pl.when(j == 0)
        def _():
            one = dot(tiles[0, 1], inverses[0], LEFT_T)
            tiles[1, 0] = tiles[1, 0] - dot(one, one, RIGHT_T)
            sides[0] = one
            two = dot(tiles[2, 1], inverses[0], RIGHT_T)
            sides[1] = two
            tiles[1, 1] = tiles[1, 1] - dot(one, two, RIGHT_T)
            tiles[2, 0] = tiles[2, 0] - dot(two, two, RIGHT_T)

        @pl.when(j == 1)
        def _():
            two = dot(tiles[1, 1], inverses[1], LEFT_T)
            sides[2] = two
            tiles[2, 0] = tiles[2, 0] - dot(two, two, RIGHT_T)

        return carry

    lax.fori_loop(0, STEPS, step, 0)


def factorize(where, mine, other):
    three = jax.ShapeDtypeStruct((STEPS, TILE, TILE), jnp.float32)
    return pl.pallas_call(
        lead_kernel,
        out_shape=(three, three, three),
        in_specs=[SMEM, VMEM, VMEM],
        out_specs=(VMEM, VMEM, VMEM),
        scratch_shapes=[
            pltpu.VMEM((STEPS, 2, TILE, TILE), jnp.float32),
            pltpu.VMEM((BLOCK, BLOCK), jnp.float32),
            pltpu.VMEM((BLOCK, BLOCK), jnp.float32),
            pltpu.VMEM((2, SUB + 2, SUB, BLOCK), jnp.float32),
        ],
        compiler_params=pltpu.CompilerParams(vmem_limit_bytes=16 * 2**20),
        cost_estimate=pl.CostEstimate(flops=3 * 10**10, bytes_accessed=10**6, transcendentals=0),
    )(where, mine, other)


def parts(value, count):
    out = []
    for _ in range(count):
        out.append(value.astype(jnp.bfloat16))
        value = value - out[-1].astype(jnp.float32)
    return out


def stack(ref, value, count):
    size = value.shape[0]
    for i, part in enumerate(parts(value, count)):
        start = size * (count - 1 - i)
        ref[start : start + size, :] = part


def times(value, ref, count):
    size = value.shape[1]
    total = None
    for i, part in reversed(list(enumerate(parts(value, count)))):
        left = jnp.concatenate([part] * (count - i), axis=1)
        product = jnp.dot(left, ref[size * i :, :], preferred_element_type=jnp.float32)
        total = product if total is None else total + product
    return total


def across_kernel(e, inverses, sides, q):
    def row(j):
        return jnp.concatenate([e[4 * s + j] for s in range(4)], axis=1)

    q0 = dot(inverses[0], row(0), NORMAL)
    stack(q.at[:LEAD], q0, 3)
    q1 = dot(inverses[1], row(1) - dot(sides[0], q0, NORMAL), NORMAL)
    q2 = row(2) - dot(sides[1], q0, NORMAL) - dot(sides[2], q1, NORMAL)
    q2 = dot(inverses[2], q2, NORMAL)
    for i, value in enumerate((q1, q2)):
        high, low = parts(value, 2)
        start = LEAD + TILE * i
        q[start : start + TILE, :] = high
        q[start + 2 * TILE : start + 3 * TILE, :] = low


def across(e, inverses, sides):
    return pl.pallas_call(
        across_kernel,
        out_shape=jax.ShapeDtypeStruct((7 * TILE, 4 * TILE), jnp.bfloat16),
        in_specs=[VMEM] * 3,
        out_specs=VMEM,
        compiler_params=pltpu.CompilerParams(vmem_limit_bytes=24 * 2**20),
        cost_estimate=pl.CostEstimate(flops=10**10, bytes_accessed=10**7, transcendentals=0),
    )(e, inverses, sides)


def update_kernel(
    where, a, mine, other, q_far, factors, inverses, sides, out,
    panel_all, block, right0, right1, rights, q, arrival
):
    r, c, core = where[0], where[1], where[2]
    t = pl.program_id(0)

    fetch = pltpu.make_async_copy(q_far, q, arrival)

    @pl.when(t == 0)
    def _():
        fetch.start()
        stack(right0, inverses[0].T, 3)
        stack(right1, jnp.concatenate([sides[0].T, sides[1].T], axis=1), 3)
        for i, value in enumerate((inverses[1], sides[2], inverses[2])):
            stack(rights.at[i], value.T, 2)

    def place(lower, upper):
        for z in range(8):
            rows = 128 * z
            block[rows : rows + 128, :TILE] = lower[z, :128]
            block[rows : rows + 128, TILE : 2 * TILE] = upper[z, :128]
            block[rows : rows + 64, 2 * TILE :] = lower[z, 128:]
            block[rows + 64 : rows + 128, 2 * TILE :] = upper[z, 128:]

    @pl.when((t == 0) & (core == 0))
    def _():
        place(mine, other)

    @pl.when((t == 0) & (core != 0))
    def _():
        place(other, mine)

    @pl.when(t == 0)
    def _():
        p0 = times(block[:, :TILE], right0, 3)
        panel_all[:, :TILE] = p0
        removed = times(p0, right1, 3)
        p1 = times(block[:, TILE : 2 * TILE] - removed[:, :TILE], rights.at[0], 2)
        panel_all[:, TILE : 2 * TILE] = p1
        p2 = block[:, 2 * TILE :] - removed[:, TILE:] - times(p1, rights.at[1], 2)
        panel_all[:, 2 * TILE :] = times(p2, rights.at[2], 2)
        fetch.wait()

    panel = panel_all.at[pl.ds(pl.multiple_of(t * TILE, TILE), TILE)]
    p0 = panel[:, :TILE]

    first, second, third = parts(p0, 3)
    high, low = parts(panel[:, TILE:], 2)
    short = lambda x, y: jnp.dot(x, y, preferred_element_type=jnp.float32)
    total = short(third, q[2 * TILE : 3 * TILE, :])
    total = total + short(jnp.concatenate([second, second, low], axis=1), q[TILE : 5 * TILE, :])
    total = total + short(jnp.concatenate([first, first, first, high, high], axis=1), q[...])
    out[...] = a[...] - total

    for k in range(STEPS):

        @pl.when(c == k)
        def _(k=k):
            out[:, :TILE] = panel[:, TILE * k : TILE * (k + 1)]

        @pl.when((t == 0) & (r == k))
        def _(k=k):
            out[:, TILE:] = jnp.zeros((TILE, 3 * TILE), jnp.float32)

            @pl.when(c == k)
            def _():
                out[:, :TILE] = factors[k]

            @pl.when(c > k)
            def _():
                out[:, :TILE] = jnp.zeros((TILE, TILE), jnp.float32)


def update(where, matrix, *operands):
    whole = lambda x: pl.BlockSpec(x.shape, lambda t: (0,) * x.ndim)
    row_tile = pl.BlockSpec((TILE, 4 * TILE), lambda t: (t, 0))
    return pl.pallas_call(
        update_kernel,
        grid=(4,),
        out_shape=jax.ShapeDtypeStruct(matrix.shape, jnp.float32),
        in_specs=[SMEM, row_tile] + [whole(x) for x in operands[:2]]
        + [pl.BlockSpec(memory_space=pl.ANY)]
        + [whole(x) for x in operands[3:]],
        out_specs=row_tile,
        scratch_shapes=[
            pltpu.VMEM((4 * TILE, LEAD), jnp.float32),
            pltpu.VMEM((4 * TILE, LEAD), jnp.float32),
            pltpu.VMEM((3 * TILE, TILE), jnp.bfloat16),
            pltpu.VMEM((3 * TILE, 2 * TILE), jnp.bfloat16),
            pltpu.VMEM((STEPS, 2 * TILE, TILE), jnp.bfloat16),
            pltpu.VMEM((7 * TILE, 4 * TILE), jnp.bfloat16),
            pltpu.SemaphoreType.DMA,
        ],
        compiler_params=pltpu.CompilerParams(vmem_limit_bytes=56 * 2**20),
        cost_estimate=pl.CostEstimate(flops=2 * 10**10, bytes_accessed=10**7, transcendentals=0),
    )(where, matrix, *operands)


def after(value, *others):
    return lax.optimization_barrier((value,) + others)[0]


def copies(value, groups):
    return jnp.broadcast_to(value[None], (len(groups[0]),) + value.shape)


def gather(copied, axis, groups):
    return lax.all_to_all(copied, axis, 0, 0, axis_index_groups=groups)


def choose(index, values):
    out = jnp.zeros_like(values[0])
    for i, value in enumerate(values):
        out = jnp.where(index == i, value, out)
    return out


def on_device(matrix):
    r = lax.axis_index("row")
    c = lax.axis_index("col")
    y, x, z, core = r // 4, r % 4, c // 2, c % 2
    where = jnp.stack([r, c, core]).astype(jnp.int32)
    swap = lambda value: lax.ppermute(value, "col", CORE_SWAP)

    def spread(values):
        sent = [lax.ppermute(values[i], "col", FAR[i]) for i in (1, 2, 3)]
        return choose(z // 2, [values[0]] + sent)

    def halves(value):
        size = value.shape[0] // 2
        keep = lax.dynamic_slice_in_dim(value, core * size, size, 0)
        got = swap(lax.dynamic_slice_in_dim(value, (1 - core) * size, size, 0))
        return jnp.stack([jnp.where(core == 0, keep, got), jnp.where(core == 0, got, keep)])

    corner, top, side = matrix[:TILE, :TILE], matrix[:TILE, :], matrix[:, :TILE]
    down = lambda value, s: lax.ppermute(value, "row", [(x0, 4 * s + x0) for x0 in range(3)])

    quarters = [corner[64 * s : 64 * (s + 1)] for s in range(4)]
    quarter = choose(y, [quarters[0]] + [down(quarters[s], s) for s in range(1, 4)])
    pair = halves(quarter)
    next_door = lax.ppermute(pair, "col", NEAR)
    t0, t1 = jnp.where(z == 0, pair, next_door)[0], jnp.where(z == 0, pair, next_door)[1]
    t2 = jnp.where(z == 0, next_door, pair)[0]
    two = spread([jnp.stack([choose(x, [t0, t1, t2]), choose(x, [t1, t2, t0])])] * 4)

    column = choose(
        y, [top[:, :TILE]] + [down(top[:, TILE * s : TILE * (s + 1)], s) for s in range(1, 4)]
    )

    chunks = after(side, two).reshape(4, 2, 128, TILE)
    sent = [chunks[0]] + [lax.ppermute(chunks[i], "col", FAR[i][:3]) for i in (1, 2, 3)]
    two, column = lax.optimization_barrier((two, column))
    e = lax.all_gather(column, "row")
    lead_mine = gather(copies(two, ROW_GROUP), "row", ROW_GROUP)

    couple = choose(z // 2, sent)
    got = lax.ppermute(jnp.where(z % 2 == 0, couple[1], couple[0]), "col", EXCHANGE)
    first = jnp.where(z % 2 == 0, couple[0], got)
    third = jnp.where(z % 2 == 0, got, couple[1])
    got = lax.ppermute(third[64:], "col", [(2 * i, 2 * i + 1) for i in range(8)])
    my_chunk = jnp.concatenate([first, jnp.where(core == 0, third[:64], got)])
    chunk_copies = copies(my_chunk, Z_GROUPS)
    lead_mine, chunk_copies, where = lax.optimization_barrier((lead_mine, chunk_copies, where))
    lead_other = swap(lead_mine)
    rows_mine = gather(chunk_copies, "col", Z_GROUPS)
    factors, inverses, sides = factorize(where, lead_mine, lead_other)
    q = across(e, inverses, sides)
    rows_mine, q = lax.optimization_barrier((rows_mine, q))
    rows_other = swap(rows_mine)
    return update(where, matrix, rows_mine, rows_other, q, factors, inverses, sides)


def solution(mesh):
    placed = (P("row", "col"),)
    return jax.shard_map(
        on_device, mesh=mesh, in_specs=placed, out_specs=P("row", "col"), check_vma=False
    )
```
